128 devices in a mesh: row: 8 (over x_hi, z), col: 16 (over x_lo, y, core).
Axes of the slice: x: 4 (x_hi: 2, x_lo: 2; x = x_hi * 2 + x_lo), y: 4, z: 4, core: 2. Of those that a mesh axis runs over, the one named last changes fastest.
Arguments:
- density_cyclic: float32 [6144, 6144], P(('row', 'col')), as said below
- mask_in: int32 [48, 48], replicated, may hold values from 0 to 1, as said below
- mask_sq: int32 [48, 48], replicated, may hold values from 0 to 1, as said below
- mask_cube: int32 [48, 48], replicated, may hold values from 0 to 1, as said below
Outputs:
- purified: float32 [6144, 6144], P('row', 'col')
- trace: float32 [], replicated
The draws below stay inside these ranges and needn't reach their ends.
Inputs may be any that keep to these rules, and one draw needn't show every extreme that they name: `density_cyclic`: density, the matrix with its rows in order, is symmetric. `mask_in`: symmetric, with ones on the diagonal. `mask_sq`: symmetric, with ones on the diagonal. `mask_cube`: symmetric, with ones on the diagonal.
All inputs are finite; a program needn't handle non-finite values.
Results may differ from the reference program's by a relative error of at most 0.00009.
Values sent between devices are 32-bit elements; how exact they have to be, the bound alone decides.
A program may use at most 128 MiB of HBM per device.

```python
import math
import jax
import jax.numpy as jnp
from jax import lax

BS = 128
NB = 48
N_ROW = 8
N_COL = 16


def symmetric_pattern(key, keep, outof):
    coins = jax.random.randint(key, (NB, NB), 0, outof)
    picked = (coins < keep).astype(jnp.int32)
    upper_rows = lax.broadcasted_iota(jnp.int32, (NB, NB), 0)
    upper_cols = lax.broadcasted_iota(jnp.int32, (NB, NB), 1)
    mirrored = jnp.where(upper_rows <= upper_cols, picked, picked.T)
    return jnp.where(upper_rows == upper_cols, 1, mirrored).astype(jnp.int32)


def draw_density_cyclic(key, part):
    key = jax.random.fold_in(key, 11)
    key_off, key_diag = jax.random.split(key)
    order = NB * BS
    devices = N_ROW * N_COL
    raw = jax.random.normal(key_off, (order, order), jnp.float32)
    spread = 0.2 / math.sqrt(order)
    off_part = (raw + raw.T) * (spread * 0.70710678)
    diag_values = jax.random.uniform(key_diag, (order,), jnp.float32, 0.3, 0.7)
    row_ids = lax.broadcasted_iota(jnp.int32, (order, order), 0)
    col_ids = lax.broadcasted_iota(jnp.int32, (order, order), 1)
    matrix = jnp.where(row_ids == col_ids, diag_values[:, None], off_part)
    per_device = order // devices
    stored = jnp.arange(order, dtype=jnp.int32)
    source = stored % per_device * devices + stored // per_device
    return matrix[source, :].astype(jnp.float32)


def draw_mask_in(key, part):
    key = jax.random.fold_in(key, 21)
    return symmetric_pattern(key, 3, 4)


def draw_mask_sq(key, part):
    key = jax.random.fold_in(key, 31)
    return symmetric_pattern(key, 7, 8)


def draw_mask_cube(key, part):
    key = jax.random.fold_in(key, 41)
    return symmetric_pattern(key, 7, 8)


def setup_inputs(seed: int = 0) -> dict:
    seeds = jax.random.split(jax.random.key(seed), 5)
    density_cyclic = draw_density_cyclic(jax.random.fold_in(seeds[4], 71), 0)
    mask_in = draw_mask_in(jax.random.fold_in(seeds[4], 71), 0)
    mask_sq = draw_mask_sq(jax.random.fold_in(seeds[4], 71), 0)
    mask_cube = draw_mask_cube(jax.random.fold_in(seeds[4], 71), 0)
    return dict(density_cyclic=density_cyclic, mask_in=mask_in, mask_sq=mask_sq, mask_cube=mask_cube)


def expand(mask):
    grown = jnp.repeat(mask.astype(jnp.float32), BS, axis=0)
    return jnp.repeat(grown, BS, axis=1)


def reference(density_cyclic, mask_in, mask_sq, mask_cube):
    order = density_cyclic.shape[1]
    devices = N_ROW * N_COL
    density = density_cyclic.reshape(devices, order // devices, order).transpose(1, 0, 2).reshape(order, order)
    filtered = density * expand(mask_in)
    square = jnp.dot(filtered, filtered, precision=lax.Precision.HIGHEST, preferred_element_type=jnp.float32)
    square = square * expand(mask_sq)
    cube = jnp.dot(square, filtered, precision=lax.Precision.HIGHEST, preferred_element_type=jnp.float32)
    cube = cube * expand(mask_cube)
    purified = 3.0 * square - 2.0 * cube
    return purified, jnp.trace(purified)
```

```python
import functools

import jax
import jax.numpy as jnp
from jax import lax
from jax.experimental import pallas as pl
from jax.experimental.pallas import tpu as pltpu
from jax.sharding import PartitionSpec as P

F32 = jnp.float32
BF16 = jnp.bfloat16
MESH = pl.DeviceIdType.MESH
BS = 128
NB = 48
HALF = 3072
KC = 4
RC = 4
ROWS = 768 // RC


def split(x):
    hi = x.astype(BF16)
    return hi, (x - hi.astype(F32)).astype(BF16)


def dot(a, b):
    return jnp.dot(a, b, preferred_element_type=F32)


def dot3(a, bh, bl):
    ah, al = split(a)
    return dot(ah, bh) + (dot(al, bh) + dot(ah, bl))


def kernel(
    t1src, t2src, msq, mcu, mdg, tr0, out, trace,
    t1recv, t2recv, acol, lhs, bhi, blo, sacc, rs1, sfull, cacc, rs2, order, tsend, trecv,
    ss, rs, ls,
):
    row = lax.axis_index("row")
    col = lax.axis_index("col")
    xh, z = row // 4, row % 4
    xl, y, c = col // 8, (col // 2) % 4, col % 2
    piece = col % 8

    def at(xh_=xh, xl_=xl, y_=y, z_=z, c_=c):
        return (xh_ * 4 + z_, (xl_ * 4 + y_) * 2 + c_)

    zp, zm, z2 = (z + 1) % 4, (z + 3) % 4, (z + 2) % 4
    yp, ym, y2 = (y + 1) % 4, (y + 3) % 4, (y + 2) % 4
    ox, ol, oc = 1 - xh, 1 - xl, 1 - c

    group1 = [
        ((xl + a) % 2, (y + b) % 4, (c + e) % 2)
        for b in (0, 1, 3, 2) for a in range(2) for e in range(2) if (a, b, e) != (0, 0, 0)
    ]
    group2 = [
        ((xh + a) % 2, (xl + b) % 2, (z + e) % 4)
        for e in (0, 1, 3, 2) for a in range(2) for b in range(2) if (a, b, e) != (0, 0, 0)
    ]
    partners = [at(xl_=a, y_=b, c_=e) for a, b, e in group1]
    partners += [at(xh_=a, xl_=b, z_=e) for i, (a, b, e) in enumerate(group2) if i != 0]

    barrier = pltpu.get_barrier_semaphore()
    for dev in partners:
        pl.semaphore_signal(barrier, inc=1, device_id=dev, device_id_type=MESH)
    pl.semaphore_wait(barrier, len(partners))

    copies = []

    def send(src, dst, dev):
        i = len(copies)
        copy = pltpu.make_async_remote_copy(
            src_ref=src, dst_ref=dst, send_sem=ss.at[i], recv_sem=rs.at[i], device_id=dev, device_id_type=MESH
        )
        copy.start()
        copies.append(copy)
        return copy

    slot1 = pl.ds(pl.multiple_of(col * 144, 8), 144)
    slot2 = pl.ds(pl.multiple_of((row * 2 + xl) * 144, 8), 144)
    own1 = pltpu.make_async_copy(t1src.at[xl, y, c], t1recv.at[slot1], ls.at[0])
    own1.start()
    own2 = pltpu.make_async_copy(t2src.at[xl, row], t2recv.at[slot2], ls.at[1])
    own2.start()
    a1, a2 = [], []
    for (a, b, e), (f, g, h) in zip(group1, group2):
        a1.append(send(t1src.at[a, b, e], t1recv.at[slot1], at(xl_=a, y_=b, c_=e)))
        a2.append(send(t2src.at[g, f * 4 + h], t2recv.at[slot2], at(xh_=f, xl_=g, z_=h)))
    own1.wait()
    for copy in a1:
        copy.wait_recv()

    def order1(blk, carry):
        for g in range(2):
            for j in range(6):
                lanes = pl.ds(j * 128, 128)
                acol[blk, row, pl.ds(g * 8, 8), lanes] = t1recv[pl.ds(g * 8 * 144 + blk * 6 + j, 8, stride=144), :]
        return carry

    lax.fori_loop(0, 24, order1, 0)

    def cols(n, slot, first=0, count=6):
        return acol.at[pl.ds(n * 6 + first, count), slot]

    def rows(n, slot):
        return lhs.at[slot, :, pl.ds(n * 768, 768)]

    g1 = [{} for _ in range(KC)]
    g2 = [{} for _ in range(KC)]

    def start1(n):
        ref = cols(n, row)
        g1[n]["x"] = send(ref, ref, at(xh_=ox))
        g1[n]["zp"] = send(ref, ref, at(z_=zp))
        g1[n]["zm"] = send(ref, ref, at(z_=zm))

    def relay1(n):
        g1[n]["x"].wait_recv()
        ref = cols(n, ox * 4 + z)
        g1[n]["qp"] = send(ref, ref, at(z_=zp))
        g1[n]["qm"] = send(ref, ref, at(z_=zm))
        g1[n]["zp"].wait_recv()
        ref = cols(n, xh * 4 + zm, 0, 3)
        g1[n]["hp"] = send(ref, ref, at(z_=zp))
        g1[n]["zm"].wait_recv()
        ref = cols(n, xh * 4 + zp, 3, 3)
        g1[n]["hm"] = send(ref, ref, at(z_=zm))

    def cross1(n):
        g1[n]["hp"].wait_recv()
        ref = cols(n, xh * 4 + z2, 0, 3)
        g1[n]["xp"] = send(ref, ref, at(xh_=ox))
        g1[n]["hm"].wait_recv()
        ref = cols(n, xh * 4 + z2, 3, 3)
        g1[n]["xm"] = send(ref, ref, at(xh_=ox))

    def end1(n):
        for key in ("qp", "qm", "xp", "xm"):
            g1[n][key].wait_recv()

    def start2(n):
        ref = rows(n, piece)
        g2[n]["c"] = send(ref, ref, at(c_=oc))
        g2[n]["yp"] = send(ref, ref, at(y_=yp))
        g2[n]["ym"] = send(ref, ref, at(y_=ym))
        g2[n]["y2"] = send(ref, ref, at(y_=y2))

    def relay2(n):
        for key, other in (("yp", ym), ("ym", yp), ("y2", y2)):
            g2[n][key].wait_recv()
            ref = rows(n, other * 2 + c)
            g2[n]["c" + key] = send(ref, ref, at(c_=oc))

    def end2(n):
        for key in ("c", "cyp", "cym", "cy2"):
            g2[n][key].wait_recv()

    start1(0)
    start1(1)
    own2.wait()
    for copy in a2:
        copy.wait_recv()

    def order2(blk, carry):
        for g in range(2):
            for j in range(24):
                start = g * 8 * 144 + blk * 24 + j
                lhs[piece, pl.ds(pl.multiple_of(blk * 16 + g * 8, 8), 8), pl.ds(j * 128, 128)] = t2recv[
                    pl.ds(start, 8, stride=144), :
                ]
        return carry

    lax.fori_loop(0, 6, order2, 0)
    start2(0)
    start2(1)

    def prepare(n):
        def body(b, carry):
            hi, lo = split(acol[n * 6 + b].reshape(BS, 768))
            at_ = pl.ds(pl.multiple_of(n * 768 + b * BS, BS), BS)
            bhi[at_, :] = hi
            blo[at_, :] = lo
            return carry

        lax.fori_loop(0, 6, body, 0)

    def square_rows(n, r):
        a = lhs[pl.ds(r * 2, 2), :, pl.ds(n * 768, 768)].reshape(ROWS, 768)
        k = pl.ds(n * 768, 768)
        got = dot3(a, bhi[k, :], blo[k, :])
        m = pl.ds(pl.multiple_of(r * ROWS, ROWS), ROWS)
        sacc[m, :] = got if n == 0 else sacc[m, :] + got

    s1 = []

    def square(n):
        prepare(n)
        if n < KC - 1:
            def body(r, carry):
                square_rows(n, r)
                return carry

            lax.fori_loop(0, RC, body, 0)
        else:
            for r in range(RC):
                square_rows(n, r)
                m = pl.ds(r * ROWS, ROWS)
                s1.append(send(sacc.at[m, pl.ds(384, 384)], rs1.at[m], at(xl_=ol)))

    for t in range(KC + 2):
        if t < KC:
            relay1(t)
            if t + 2 < KC:
                start1(t + 2)
            relay2(t)
            if t + 2 < KC:
                start2(t + 2)
        if 0 <= t - 1 < KC:
            cross1(t - 1)
        if 0 <= t - 2 < KC:
            end1(t - 2)
            end2(t - 2)
            square(t - 2)

    mine = pl.multiple_of(piece * 384, 128)
    g3 = [{} for _ in range(RC)]
    s2 = [None] * RC
    total = [tr0[...]]

    def begin3(r):
        m = pl.ds(r * ROWS, ROWS)
        s1[r].wait_recv()
        s = (sacc[m, pl.ds(0, 384)] + rs1[m, :]).reshape(2, 6, 16, 384) * msq[...][None]
        sfull[piece, m, :] = s.reshape(ROWS, 384)
        ref = sfull.at[piece, m]
        g3[r]["yp"] = send(ref, ref, at(y_=yp))
        g3[r]["ym"] = send(ref, ref, at(y_=ym))
        g3[r]["c"] = send(ref, ref, at(c_=oc))
        a = lhs[pl.ds(r * 2, 2), :, pl.ds(mine, 384)].reshape(2, 6, 16, 384)
        part = jnp.sum((s * a * mdg[...][None]).reshape(24, 8, 384), axis=0)
        total[0] = total[0] - 2.0 * (part[:, 0:128] + part[:, 128:256] + part[:, 256:384])

    def relay3(r):
        m = pl.ds(r * ROWS, ROWS)
        g3[r]["yp"].wait_recv()
        ref = sfull.at[ym * 2 + c, pl.ds(r * ROWS, ROWS // 2)]
        g3[r]["hp"] = send(ref, ref, at(y_=yp))
        ref = sfull.at[ym * 2 + c, m]
        g3[r]["cyp"] = send(ref, ref, at(c_=oc))
        g3[r]["ym"].wait_recv()
        ref = sfull.at[yp * 2 + c, pl.ds(r * ROWS + ROWS // 2, ROWS // 2)]
        g3[r]["hm"] = send(ref, ref, at(y_=ym))
        ref = sfull.at[yp * 2 + c, m]
        g3[r]["cym"] = send(ref, ref, at(c_=oc))

    def far3(r):
        g3[r]["hp"].wait_recv()
        ref = sfull.at[y2 * 2 + c, pl.ds(r * ROWS, ROWS // 2)]
        g3[r]["chp"] = send(ref, ref, at(c_=oc))
        g3[r]["hm"].wait_recv()
        ref = sfull.at[y2 * 2 + c, pl.ds(r * ROWS + ROWS // 2, ROWS // 2)]
        g3[r]["chm"] = send(ref, ref, at(c_=oc))

    def cube(r):
        m = pl.ds(r * ROWS, ROWS)
        for key in ("c", "cyp", "cym", "chp", "chm"):
            g3[r][key].wait_recv()

        def body(s, carry):
            k = pl.ds(pl.multiple_of(s * 384, 384), 384)
            cacc[m, :] = cacc[m, :] + dot3(sfull[s, m, :], bhi[k, :], blo[k, :])
            return carry

        cacc[m, :] = jnp.zeros((ROWS, 768), F32)
        lax.fori_loop(0, 8, body, 0)
        s2[r] = send(cacc.at[m, pl.ds(384, 384)], rs2.at[m], at(xl_=ol))

    def finish(r):
        m = pl.ds(r * ROWS, ROWS)
        s2[r].wait_recv()
        got = (cacc[m, pl.ds(0, 384)] + rs2[m, :]).reshape(2, 6, 16, 384) * mcu[...][None]
        got = 3.0 * sfull[piece, m, :] - 2.0 * got.reshape(ROWS, 384)
        for i in range(2):
            for j in range(3):
                order[pl.ds(j * 768 + r * 2 + i, 96, stride=8), :] = got[
                    i * 96:(i + 1) * 96, j * 128:(j + 1) * 128
                ]

    steps = [at(c_=oc), at(xl_=ol), at(xh_=ox), at(y_=y + 1 - 2 * (y % 2)), at(z_=z + 1 - 2 * (z % 2)), at(y_=y2), at(z_=z2)]
    flying = []

    def trace_step():
        if flying:
            n, copy = flying.pop()
            copy.wait_recv()
            total[0] = total[0] + trecv[n]
            if n + 1 == len(steps):
                trace[...] = total[0]
                return
            n = n + 1
        else:
            n = 0
        if n >= len(steps):
            return
        tsend[n] = total[0]
        flying.append((n, send(tsend.at[n], trecv.at[n], steps[n])))

    left = len(steps) + 1

    def advance(t):
        nonlocal left
        if t >= RC and left:
            trace_step()
            left -= 1

    for t in range(RC + 4):
        if t < RC:
            begin3(t)
        advance(t)
        if 0 <= t - 1 < RC:
            relay3(t - 1)
            advance(t)
        if 0 <= t - 2 < RC:
            far3(t - 2)
            advance(t)
        if 0 <= t - 3 < RC:
            cube(t - 3)
            advance(t)
        if 0 <= t - 4 < RC:
            finish(t - 4)
    for j in range(3):
        out[:, pl.ds(j * 128, 128)] = order[pl.ds(j * 768, 768), :]
    while left:
        trace_step()
        left -= 1
    assert len(copies) == N_COPIES
    for copy in copies:
        copy.wait_send()


N_COPIES = 30 + KC * 16 + RC * 11 + 7


def call(t1src, t2src, msq, mcu, mdg, tr0):
    vmem = pl.BlockSpec(memory_space=pltpu.VMEM)
    hbm = pl.BlockSpec(memory_space=pl.ANY)
    return pl.pallas_call(
        kernel,
        out_shape=(jax.ShapeDtypeStruct((768, 384), F32), jax.ShapeDtypeStruct((8, 128), F32)),
        in_specs=[hbm, hbm, vmem, vmem, vmem, vmem],
        out_specs=(vmem, vmem),
        scratch_shapes=[
            pltpu.VMEM((2304, 128), F32),
            pltpu.VMEM((2304, 128), F32),
            pltpu.VMEM((24, 8, 16, 768), F32),
            pltpu.VMEM((8, 96, HALF), F32),
            pltpu.VMEM((HALF, 768), BF16),
            pltpu.VMEM((HALF, 768), BF16),
            pltpu.VMEM((768, 768), F32),
            pltpu.VMEM((768, 384), F32),
            pltpu.VMEM((8, 768, 384), F32),
            pltpu.VMEM((768, 768), F32),
            pltpu.VMEM((768, 384), F32),
            pltpu.VMEM((2304, 128), F32),
            pltpu.VMEM((7, 8, 128), F32),
            pltpu.VMEM((7, 8, 128), F32),
            pltpu.SemaphoreType.DMA((N_COPIES,)),
            pltpu.SemaphoreType.DMA((N_COPIES,)),
            pltpu.SemaphoreType.DMA((2,)),
        ],
        compiler_params=pltpu.CompilerParams(
            collective_id=0, has_side_effects=True, vmem_limit_bytes=62 * 2**20
        ),
        cost_estimate=pl.CostEstimate(flops=2 * 768 * 768 * HALF * 6, bytes_accessed=4 * 2**20, transcendentals=0),
    )(t1src, t2src, msq, mcu, mdg, tr0)


def shards(density_cyclic, mask_in, mask_sq, mask_cube):
    row = lax.axis_index("row")
    col = lax.axis_index("col")
    pm = density_cyclic.reshape(NB, NB, BS) * mask_in.astype(F32)[:, :, None]
    t2src = pm.reshape(8, 6, 2, 24, BS).transpose(2, 0, 1, 3, 4).reshape(2, 8, 144, BS)
    both = pm.reshape(2, 24, 2, 4, 2, 384)
    both = jnp.stack([both[0], both[1][:, ::-1]])
    t1src = both.transpose(0, 3, 4, 1, 2, 5).reshape(2, 4, 2, 144, BS)

    def tile(mask):
        piece = lax.dynamic_slice(mask, (row * 6, col * 3), (6, 3)).astype(F32)
        return jnp.broadcast_to(piece[:, None, :, None], (6, 16, 3, BS)).reshape(6, 16, 384)

    mdiag = lax.dynamic_slice(jnp.diagonal(mask_cube), (row * 6,), (6,)).astype(F32)
    mdg = jnp.broadcast_to(mdiag[:, None, None], (6, 16, 384))
    weight = jnp.diagonal(mask_sq).astype(F32)[:, None, None]
    tr0 = 3.0 * jnp.sum((pm * pm * weight).reshape(NB * 6, 8, BS), axis=0)
    purified, trace = call(t1src, t2src, tile(mask_sq), tile(mask_cube), mdg, tr0)
    return purified, jnp.sum(trace)


def solution(mesh):
    in_specs = (P(("row", "col"), None), P(), P(), P())
    out_specs = (P("row", "col"), P())
    return jax.shard_map(shards, mesh=mesh, in_specs=in_specs, out_specs=out_specs, check_vma=False)
```

```python
import jax
import jax.numpy as jnp
from jax import lax
from jax.experimental import pallas as pl
from jax.experimental.pallas import tpu as pltpu
from jax.sharding import PartitionSpec as P

F32 = jnp.float32
BF16 = jnp.bfloat16
MESH = pl.DeviceIdType.MESH
BS = 128
NB = 48
HALF = 3072
OWN, OTHER = 0, 1
CHUNKS = ((OTHER, 0, "x"), (OTHER, 1, "x"), (OWN, 0, "z"), (OWN, 1, "z"))
RC = 8
ROWS = 768 // RC
PIECES = 8 // RC


def split(x):
    hi = x.astype(BF16)
    return hi, (x - hi.astype(F32)).astype(BF16)


def dot(a, b):
    return jnp.dot(a, b, preferred_element_type=F32)


def dot3(a, bh, bl):
    ah, al = split(a)
    return dot(ah, bh) + (dot(al, bh) + dot(ah, bl))


def kernel(
    den, mask_in, mask_sq, mask_cube, out, trace,
    local, t1recv, t2src, t2mid, t2recv, flat, acol, lhs, bhi, blo, so, sw, rs1, sfull, cacc, rs2, tacc, tone, ttwo,
    ss, rs, ls,
):
    row = lax.axis_index("row")
    col = lax.axis_index("col")
    xh, z = row // 4, row % 4
    xl, y, c = col // 8, (col // 2) % 4, col % 2
    piece = col % 8

    def at(xh_=xh, xl_=xl, y_=y, z_=z, c_=c):
        return (xh_ * 4 + z_, (xl_ * 4 + y_) * 2 + c_)

    zp, zm, z2 = (z + 1) % 4, (z + 3) % 4, (z + 2) % 4
    yp, ym, y2 = (y + 1) % 4, (y + 3) % 4, (y + 2) % 4
    ox, ol, oc = 1 - xh, 1 - xl, 1 - c

    group1 = [
        ((xl + a) % 2, (y + b) % 4, (c + e) % 2)
        for b in (2, 1, 3, 0) for a in (1, 0) for e in range(2) if (a, b, e) != (0, 0, 0)
    ]
    crosses = [((xh + a) % 2, (xl + b) % 2) for a, b in ((1, 0), (1, 1), (0, 1))]
    partners = [at(xl_=a, y_=b, c_=e) for a, b, e in group1]
    partners += [at(xh_=a, z_=b) for a, b in ((xh, zp), (xh, zm), (ox, z), (xh, z2), (ox, zp), (ox, zm), (ox, z2))]
    partners.append(at(xh_=ox, xl_=ol))

    stage = pltpu.make_async_copy(den, local, ls.at[0])
    stage.start()
    barrier = pltpu.get_barrier_semaphore()
    for dev in partners:
        pl.semaphore_signal(barrier, inc=1, device_id=dev, device_id_type=MESH)
    stage.wait()

    def spread(b, carry):
        for j in range(NB):
            first = (j // 24 * NB + b * 8) * 24 + j % 24
            t2src[pl.ds(first, 8, stride=24), :] = local[pl.ds(pl.multiple_of(b * 8, 8), 8), pl.ds(j * BS, BS)]
        return carry

    lax.fori_loop(0, 6, spread, 0)
    pl.semaphore_wait(barrier, len(partners))

    copies = []

    def send(src, dst, dev):
        i = len(copies)
        copy = pltpu.make_async_remote_copy(
            src_ref=src, dst_ref=dst, send_sem=ss.at[i], recv_sem=rs.at[i], device_id=dev, device_id_type=MESH
        )
        copy.start()
        copies.append(copy)
        return copy

    def part1(h, a, b, e):
        half = a if h == OWN else 1 - a
        first = (half * 4 + b) * 768 + e * 384
        return den.at[pl.ds(pl.multiple_of(a * 24, 8), 24), pl.ds(pl.multiple_of(first, 128), 384)]

    def lines(n):
        return pl.ds(pl.multiple_of(n * 144, 8), 144)

    def part2(a, b, e):
        return t2src.at[lines(b * 8 + a * 4 + e)]

    def mid2(a, b, e):
        return t2mid.at[lines((a * 2 + b) * 4 + e)]

    own1, a1 = [None, None], [None, None]

    def deal1(h):
        own1[h] = pltpu.make_async_copy(part1(h, xl, y, c), t1recv.at[h, col], ls.at[1 + h])
        own1[h].start()
        a1[h] = [send(part1(h, a, b, e), t1recv.at[h, col], at(xl_=a, y_=b, c_=e)) for a, b, e in group1]

    a2, b2, own2 = [], [], []

    def deal2():
        for a in range(2):
            for b in range(2):
                copy = pltpu.make_async_copy(part2(a, b, z), mid2(a, b, z), ls.at[3 + a * 2 + b])
                copy.start()
                own2.append(copy)
                for e in (z2, zp, zm):
                    a2.append(send(part2(a, b, e), mid2(a, b, z), at(z_=e)))

    def cross2():
        for copy in own2:
            copy.wait()
        for copy in a2:
            copy.wait_recv()
        own2.clear()
        for n in range(4):
            there = lines((xh * 4 + n) * 2 + xl)
            copy = pltpu.make_async_copy(mid2(xh, xl, n), t2recv.at[there], ls.at[7 + n])
            copy.start()
            own2.append(copy)
            for a, b in crosses:
                b2.append(send(mid2(a, b, n), t2recv.at[there], at(xh_=a, xl_=b)))

    def arrive1(h):
        own1[h].wait()
        for copy in a1[h]:
            copy.wait_recv()
        for j in range(3):
            flat[pl.ds(j * 384, 384), :] = t1recv[h, :, :, pl.ds(j * BS, BS)].reshape(384, BS)
        block = ((xl if h == OWN else ol) * 4 + y) * 6 + c * 3

        def body(b, carry):
            for j in range(3):
                keep = mask_in[xl * 24 + b, block + j].astype(F32)
                for g in range(2):
                    got = flat[pl.ds(j * 384 + g * 192 + b, 8, stride=24), :] * keep
                    acol[b, row, pl.ds(g * 8, 8), pl.ds(h * 384 + j * BS, BS)] = got
            return carry

        lax.fori_loop(0, 24, body, 0)

    def arrive2():
        for copy in own2:
            copy.wait()
        for copy in b2:
            copy.wait_recv()

        def body(b, carry):
            for j in range(24):
                keep = mask_in[row * 6 + b, xl * 24 + j].astype(F32)
                for g in range(2):
                    got = t2recv[pl.ds(g * 8 * 144 + b * 24 + j, 8, stride=144), :] * keep
                    lhs[piece, pl.ds(pl.multiple_of(b * 16 + g * 8, 8), 8), pl.ds(j * BS, BS)] = got
            return carry

        lax.fori_loop(0, 6, body, 0)

    g1 = [{} for _ in CHUNKS]

    def cols(n, slot, part=None):
        h, k, _ = CHUNKS[n]
        first, count = (k * 12, 12) if part is None else (k * 12 + part * 6, 6)
        return acol.at[pl.ds(first, count), slot, :, pl.ds(h * 384, 384)]

    def pass1(n, key, ref, dev):
        g1[n][key] = send(ref, ref, dev)

    def start1(n):
        pass1(n, "x", cols(n, row), at(xh_=ox))
        pass1(n, "zp", cols(n, row), at(z_=zp))
        pass1(n, "zm", cols(n, row), at(z_=zm))

    def relay1(n):
        g1[n]["x"].wait_recv()
        pass1(n, "qp", cols(n, ox * 4 + z), at(z_=zp))
        pass1(n, "qm", cols(n, ox * 4 + z), at(z_=zm))
        g1[n]["zp"].wait_recv()
        pass1(n, "hp", cols(n, xh * 4 + zm, 0), at(z_=zp))
        g1[n]["zm"].wait_recv()
        pass1(n, "hm", cols(n, xh * 4 + zp, 1), at(z_=zm))

    def cross1(n):
        if CHUNKS[n][2] == "x":
            g1[n]["hp"].wait_recv()
            pass1(n, "fp", cols(n, xh * 4 + z2, 0), at(xh_=ox))
            g1[n]["hm"].wait_recv()
            pass1(n, "fm", cols(n, xh * 4 + z2, 1), at(xh_=ox))
        else:
            g1[n]["qp"].wait_recv()
            pass1(n, "fp", cols(n, ox * 4 + zm, 0), at(z_=zp))
            g1[n]["qm"].wait_recv()
            pass1(n, "fm", cols(n, ox * 4 + zp, 1), at(z_=zm))

    def end1(n):
        for key in ("qp", "qm") if CHUNKS[n][2] == "x" else ("hp", "hm"):
            g1[n][key].wait_recv()
        for key in ("fp", "fm"):
            g1[n][key].wait_recv()
        h, k, _ = CHUNKS[n]
        lanes = pl.ds(h * 384, 384)

        def body(b, carry):
            hi, lo = split(acol[b, :, :, lanes].reshape(BS, 384))
            at_ = pl.ds(pl.multiple_of(b * BS, BS), BS)
            bhi[at_, lanes] = hi
            blo[at_, lanes] = lo
            return carry

        lax.fori_loop(k * 12, k * 12 + 12, body, 0)

    g2 = [{}, {}]

    def rows(n, slot, part=None):
        where = slice(None) if part is None else pl.ds(part * 48, 48)
        return lhs.at[slot, where, pl.ds(n * 1536, 1536)]

    def pass2(n, key, ref, dev):
        g2[n][key] = send(ref, ref, dev)

    def start2(n):
        pass2(n, "yp", rows(n, piece), at(y_=yp))
        pass2(n, "ym", rows(n, piece), at(y_=ym))
        pass2(n, "c", rows(n, piece), at(c_=oc))

    def relay2(n):
        g2[n]["yp"].wait_recv()
        pass2(n, "hp", rows(n, ym * 2 + c, 0), at(y_=yp))
        pass2(n, "cyp", rows(n, ym * 2 + c), at(c_=oc))
        g2[n]["ym"].wait_recv()
        pass2(n, "hm", rows(n, yp * 2 + c, 1), at(y_=ym))
        pass2(n, "cym", rows(n, yp * 2 + c), at(c_=oc))

    def far2(n):
        g2[n]["hp"].wait_recv()
        pass2(n, "chp", rows(n, y2 * 2 + c, 0), at(c_=oc))
        g2[n]["hm"].wait_recv()
        pass2(n, "chm", rows(n, y2 * 2 + c, 1), at(c_=oc))

    def end2(n):
        for key in ("c", "cyp", "cym", "chp", "chm"):
            g2[n][key].wait_recv()

    s1 = []

    def other(there):
        m = pl.ds(there * 192, 192)
        lanes = pl.ds(384, 384)
        for n in range(2):
            k = pl.ds(n * 1536, 1536)
            got = dot3(lhs[pl.ds(there * 2, 2), :, k].reshape(192, 1536), bhi[k, lanes], blo[k, lanes])
            so[m, :] = got if n == 0 else so[m, :] + got
        s1.append(send(so.at[m], rs1.at[m], at(xl_=ol)))

    def own_rows(r, n):
        k = pl.ds(n * 1536, 1536)
        a = lhs[pl.ds(r * PIECES, PIECES), :, k].reshape(ROWS, 1536)
        return dot3(a, bhi[k, pl.ds(0, 384)], blo[k, pl.ds(0, 384)])

    deal1(OTHER)
    deal2()
    arrive1(OTHER)
    start1(0)
    start1(1)
    deal1(OWN)
    cross2()
    relay1(0)
    arrive1(OWN)
    arrive2()
    start2(0)
    start2(1)
    relay1(1)
    start1(2)
    cross1(0)
    relay2(0)
    relay1(2)
    start1(3)
    cross1(1)
    end1(0)
    relay2(1)
    far2(0)
    end1(1)
    cross1(2)
    far2(1)
    end2(0)
    end2(1)
    other(0)
    relay1(3)
    other(1)
    end1(2)
    other(2)
    other(3)

    def first_half(i, carry):
        m = pl.ds(pl.multiple_of(i * 192, 64), 192)
        k = pl.ds(0, 1536)
        a = lhs[pl.ds(i * 2, 2), :, k].reshape(192, 1536)
        sw[m, :] = dot3(a, bhi[k, pl.ds(0, 384)], blo[k, pl.ds(0, 384)])
        return carry

    lax.fori_loop(0, 2, first_half, 0)
    cross1(3)
    lax.fori_loop(2, 4, first_half, 0)
    end1(3)

    mine = pl.multiple_of(piece * 384, 128)
    block = col * 3
    keep_sq = [[mask_sq[row * 6 + b, block + j].astype(F32) for j in range(3)] for b in range(6)]
    keep_cube = [[mask_cube[row * 6 + b, block + j].astype(F32) for j in range(3)] for b in range(6)]
    diag_sq = [3.0 * mask_sq[row * 6 + b, row * 6 + b].astype(F32) for b in range(6)]
    diag_cube = [2.0 * mask_cube[row * 6 + b, row * 6 + b].astype(F32) for b in range(6)]
    g3 = [{} for _ in range(RC)]
    s2 = [None] * RC

    def pass3(r, key, ref, dev):
        g3[r][key] = send(ref, ref, dev)

    def begin3(r):
        m = pl.ds(r * ROWS, ROWS)
        got = own_rows(r, 1) + sw[m, :]
        if r % (RC // 4) == 0:
            s1[r * 4 // RC].wait_recv()
        got = got + rs1[m, :]
        total = jnp.zeros((8, BS), F32)
        for i in range(PIECES):
            for b in range(6):
                for j in range(3):
                    first, lanes = i * 96 + b * 16, pl.ds(j * BS, BS)
                    s = got[first:first + 16, j * BS:(j + 1) * BS] * keep_sq[b][j]
                    sfull[piece, pl.ds(r * ROWS + first, 16), lanes] = s
                    a = lhs[r * PIECES + i, pl.ds(b * 16, 16), pl.ds(pl.multiple_of(mine + j * BS, BS), BS)]
                    part = a * (a * diag_sq[b] - s * diag_cube[b])
                    total = total + part[0:8] + part[8:16]
        tacc[...] = total if r == 0 else tacc[...] + total
        ref = sfull.at[piece, m]
        pass3(r, "yp", ref, at(y_=yp))
        pass3(r, "ym", ref, at(y_=ym))
        pass3(r, "c", ref, at(c_=oc))

    def square(r, slot, part=None):
        first, count = (r * ROWS, ROWS) if part is None else (r * ROWS + part * (ROWS // 2), ROWS // 2)
        return sfull.at[slot, pl.ds(first, count)]

    def relay3(r):
        g3[r]["yp"].wait_recv()
        pass3(r, "hp", square(r, ym * 2 + c, 0), at(y_=yp))
        pass3(r, "cyp", square(r, ym * 2 + c), at(c_=oc))
        g3[r]["ym"].wait_recv()
        pass3(r, "hm", square(r, yp * 2 + c, 1), at(y_=ym))
        pass3(r, "cym", square(r, yp * 2 + c), at(c_=oc))

    def far3(r):
        g3[r]["hp"].wait_recv()
        pass3(r, "chp", square(r, y2 * 2 + c, 0), at(c_=oc))
        g3[r]["hm"].wait_recv()
        pass3(r, "chm", square(r, y2 * 2 + c, 1), at(c_=oc))

    def cube(r):
        m = pl.ds(r * ROWS, ROWS)
        for key in ("c", "cyp", "cym", "chp", "chm"):
            g3[r][key].wait_recv()

        def body(s, carry):
            k = pl.ds(pl.multiple_of(s * 384, 384), 384)
            cacc[m, :] = cacc[m, :] + dot3(sfull[s, m, :], bhi[k, :], blo[k, :])
            return carry

        cacc[m, :] = jnp.zeros((ROWS, 768), F32)
        lax.fori_loop(0, 8, body, 0)
        s2[r] = send(cacc.at[m, pl.ds(384, 384)], rs2.at[m], at(xl_=ol))

    def finish(r):
        m = pl.ds(r * ROWS, ROWS)
        s2[r].wait_recv()
        got = cacc[m, pl.ds(0, 384)] + rs2[m, :]
        for i in range(PIECES):
            for j in range(3):
                parts = []
                for b in range(6):
                    first = i * 96 + b * 16
                    parts.append(got[first:first + 16, j * BS:(j + 1) * BS] * (2.0 * keep_cube[b][j]))
                s = sfull[piece, pl.ds(r * ROWS + i * 96, 96), pl.ds(j * BS, BS)]
                flat2 = 3.0 * s - jnp.concatenate(parts, axis=0)
                t2recv[pl.ds(j * 768 + r * PIECES + i, 96, stride=8), :] = flat2

    across = [at(xl_=a, y_=b, c_=e) for a, b, e in group1]
    along = [at(xh_=a, z_=b) for a, b in ((xh, zp), (xh, zm), (ox, z), (xh, z2), (ox, zp), (ox, zm), (ox, z2))]
    sums = []

    def trace_first():
        tone[col] = tacc[...]
        sums.append([send(tone.at[col], tone.at[col], dev) for dev in across])

    def trace_second():
        for copy in sums[0]:
            copy.wait_recv()
        ttwo[row] = jnp.sum(tone[...], axis=0)
        sums.append([send(ttwo.at[row], ttwo.at[row], dev) for dev in along])

    def trace_third():
        for copy in sums[1]:
            copy.wait_recv()
        trace[0, 0] = jnp.sum(ttwo[...])

    begin3(0)
    begin3(1)
    for t in range(RC + 3):
        if t < RC:
            relay3(t)
        if t + 2 < RC:
            begin3(t + 2)
        if 0 <= t - 1 < RC:
            far3(t - 1)
        if t == RC - 2:
            trace_first()
        if 0 <= t - 2 < RC:
            cube(t - 2)
        if t == RC + 1:
            trace_second()
        if 0 <= t - 3 < RC:
            finish(t - 3)
    for j in range(3):
        out[:, pl.ds(j * BS, BS)] = t2recv[pl.ds(j * 768, 768), :]
    trace_third()
    assert len(copies) == N_COPIES
    for copy in copies:
        copy.wait_send()


N_COPIES = 54 + 9 * len(CHUNKS) + 2 * 9 + 4 + RC * 10 + 22


def call(den, mask_in, mask_sq, mask_cube):
    vmem = pl.BlockSpec(memory_space=pltpu.VMEM)
    smem = pl.BlockSpec(memory_space=pltpu.SMEM)
    return pl.pallas_call(
        kernel,
        out_shape=(jax.ShapeDtypeStruct((768, 384), F32), jax.ShapeDtypeStruct((1, 1), F32)),
        in_specs=[pl.BlockSpec(memory_space=pl.ANY), smem, smem, smem],
        out_specs=(vmem, smem),
        scratch_shapes=[
            pltpu.VMEM((NB, 6144), F32),
            pltpu.VMEM((2, 16, 24, 384), F32),
            pltpu.VMEM((2304, BS), F32),
            pltpu.VMEM((2304, BS), F32),
            pltpu.VMEM((2304, BS), F32),
            pltpu.VMEM((1152, BS), F32),
            pltpu.VMEM((24, 8, 16, 768), F32),
            pltpu.VMEM((8, 96, HALF), F32),
            pltpu.VMEM((HALF, 768), BF16),
            pltpu.VMEM((HALF, 768), BF16),
            pltpu.VMEM((768, 384), F32),
            pltpu.VMEM((768, 384), F32),
            pltpu.VMEM((768, 384), F32),
            pltpu.VMEM((8, 768, 384), F32),
            pltpu.VMEM((768, 768), F32),
            pltpu.VMEM((768, 384), F32),
            pltpu.VMEM((8, BS), F32),
            pltpu.VMEM((16, 8, BS), F32),
            pltpu.VMEM((8, 8, BS), F32),
            pltpu.SemaphoreType.DMA((N_COPIES,)),
            pltpu.SemaphoreType.DMA((N_COPIES,)),
            pltpu.SemaphoreType.DMA((11,)),
        ],
        compiler_params=pltpu.CompilerParams(
            collective_id=0, has_side_effects=True, vmem_limit_bytes=62 * 2**20
        ),
        cost_estimate=pl.CostEstimate(flops=2 * 768 * 768 * HALF * 6, bytes_accessed=4 * 2**20, transcendentals=0),
    )(den, mask_in, mask_sq, mask_cube)


def shards(density_cyclic, mask_in, mask_sq, mask_cube):
    purified, trace = call(density_cyclic, mask_in, mask_sq, mask_cube)
    return purified, trace[0, 0]


def solution(mesh):
    in_specs = (P(("row", "col"), None), P(), P(), P())
    out_specs = (P("row", "col"), P())
    return jax.shard_map(shards, mesh=mesh, in_specs=in_specs, out_specs=out_specs, check_vma=False)
```

```python
import jax
import jax.numpy as jnp
from jax import lax
from jax.experimental import pallas as pl
from jax.experimental.pallas import tpu as pltpu
from jax.sharding import PartitionSpec as P

F32 = jnp.float32
BF16 = jnp.bfloat16
MESH = pl.DeviceIdType.MESH
BS = 128
NB = 48
HALF = 3072
OWN, OTHER = 0, 1
CHUNKS = ((OTHER, 0, "x"), (OTHER, 1, "x"), (OWN, 0, "z"), (OWN, 1, "z"))
RC = 8
ROWS = 768 // RC
PIECES = 8 // RC


def split(x):
    hi = x.astype(BF16)
    return hi, (x - hi.astype(F32)).astype(BF16)


def dot(a, b):
    return jnp.dot(a, b, preferred_element_type=F32)


def dot3(a, bh, bl):
    ah, al = split(a)
    n = a.shape[0]
    both = dot(jnp.concatenate([ah, al], axis=0), bh)
    return both[:n] + (both[n:] + dot(ah, bl))


def kernel(
    den, mask_in, mask_sq, mask_cube, out, trace,
    local, t1recv, t2src, t2recv, flat, acol, lhs, bhi, blo, so, sw, rs1, sfull, cacc, rs2, tacc, tone, ttwo,
    ss, rs, ls,
):
    row = lax.axis_index("row")
    col = lax.axis_index("col")
    xh, z = row // 4, row % 4
    xl, y, c = col // 8, (col // 2) % 4, col % 2
    piece = col % 8

    def at(xh_=xh, xl_=xl, y_=y, z_=z, c_=c):
        return (xh_ * 4 + z_, (xl_ * 4 + y_) * 2 + c_)

    zp, zm, z2 = (z + 1) % 4, (z + 3) % 4, (z + 2) % 4
    yp, ym, y2 = (y + 1) % 4, (y + 3) % 4, (y + 2) % 4
    ox, ol, oc = 1 - xh, 1 - xl, 1 - c

    group1 = [
        ((xl + a) % 2, (y + b) % 4, (c + e) % 2)
        for b in (2, 1, 3, 0) for a in (1, 0) for e in range(2) if (a, b, e) != (0, 0, 0)
    ]
    group2 = [
        ((xh + a) % 2, (xl + b) % 2, (z + e) % 4)
        for e in (2, 1, 3, 0) for a in (1, 0) for b in (1, 0) if (a, b, e) != (0, 0, 0)
    ]
    partners = [at(xl_=a, y_=b, c_=e) for a, b, e in group1]
    partners += [at(xh_=a, xl_=b, z_=e) for a, b, e in group2[:-1]]

    stage = pltpu.make_async_copy(den, local, ls.at[0])
    stage.start()
    barrier = pltpu.get_barrier_semaphore()
    for dev in partners:
        pl.semaphore_signal(barrier, inc=1, device_id=dev, device_id_type=MESH)
    stage.wait()

    def spread(b, carry):
        for j in range(NB):
            first = (j // 24 * NB + b * 8) * 24 + j % 24
            t2src[pl.ds(first, 8, stride=24), :] = local[pl.ds(pl.multiple_of(b * 8, 8), 8), pl.ds(j * BS, BS)]
        return carry

    lax.fori_loop(0, 6, spread, 0)
    pl.semaphore_wait(barrier, len(partners))

    copies = []

    def send(src, dst, dev):
        i = len(copies)
        copy = pltpu.make_async_remote_copy(
            src_ref=src, dst_ref=dst, send_sem=ss.at[i], recv_sem=rs.at[i], device_id=dev, device_id_type=MESH
        )
        copy.start()
        copies.append(copy)
        return copy

    def part1(h, a, b, e):
        half = a if h == OWN else 1 - a
        first = (half * 4 + b) * 768 + e * 384
        return den.at[pl.ds(pl.multiple_of(a * 24, 8), 24), pl.ds(pl.multiple_of(first, 128), 384)]

    def lines(n):
        return pl.ds(pl.multiple_of(n * 144, 8), 144)

    def part2(a, b, e):
        return t2src.at[lines(b * 8 + a * 4 + e)]

    own1, a1 = [None, None], [None, None]

    def deal1(h):
        own1[h] = pltpu.make_async_copy(part1(h, xl, y, c), t1recv.at[h, col], ls.at[1 + h])
        own1[h].start()
        a1[h] = [send(part1(h, a, b, e), t1recv.at[h, col], at(xl_=a, y_=b, c_=e)) for a, b, e in group1]

    a2, own2 = [], []

    def deal2():
        there = lines(row * 2 + xl)
        own2.append(pltpu.make_async_copy(part2(xh, xl, z), t2recv.at[there], ls.at[3]))
        own2[0].start()
        for a, b, e in group2:
            a2.append(send(part2(a, b, e), t2recv.at[there], at(xh_=a, xl_=b, z_=e)))

    def arrive1(h):
        own1[h].wait()
        for copy in a1[h]:
            copy.wait_recv()
        for j in range(3):
            flat[pl.ds(j * 384, 384), :] = t1recv[h, :, :, pl.ds(j * BS, BS)].reshape(384, BS)
        block = ((xl if h == OWN else ol) * 4 + y) * 6 + c * 3

        def body(b, carry):
            for j in range(3):
                keep = mask_in[xl * 24 + b, block + j].astype(F32)
                for g in range(2):
                    got = flat[pl.ds(j * 384 + g * 192 + b, 8, stride=24), :] * keep
                    acol[b, row, pl.ds(g * 8, 8), pl.ds(h * 384 + j * BS, BS)] = got
            return carry

        lax.fori_loop(0, 24, body, 0)

    def arrive2():
        for copy in own2:
            copy.wait()
        for copy in a2:
            copy.wait_recv()

        def body(b, carry):
            for j in range(24):
                keep = mask_in[row * 6 + b, xl * 24 + j].astype(F32)
                for g in range(2):
                    got = t2recv[pl.ds(g * 8 * 144 + b * 24 + j, 8, stride=144), :] * keep
                    lhs[piece, pl.ds(pl.multiple_of(b * 16 + g * 8, 8), 8), pl.ds(j * BS, BS)] = got
            return carry

        lax.fori_loop(0, 6, body, 0)

    g1 = [{} for _ in CHUNKS]

    def cols(n, slot, part=None):
        h, k, _ = CHUNKS[n]
        first, count = (k * 12, 12) if part is None else (k * 12 + part * 6, 6)
        return acol.at[pl.ds(first, count), slot, :, pl.ds(h * 384, 384)]

    def pass1(n, key, ref, dev):
        g1[n][key] = send(ref, ref, dev)

    def start1(n):
        pass1(n, "x", cols(n, row), at(xh_=ox))
        pass1(n, "zp", cols(n, row), at(z_=zp))
        pass1(n, "zm", cols(n, row), at(z_=zm))

    def relay1(n):
        g1[n]["x"].wait_recv()
        pass1(n, "qp", cols(n, ox * 4 + z), at(z_=zp))
        pass1(n, "qm", cols(n, ox * 4 + z), at(z_=zm))
        g1[n]["zp"].wait_recv()
        pass1(n, "hp", cols(n, xh * 4 + zm, 0), at(z_=zp))
        g1[n]["zm"].wait_recv()
        pass1(n, "hm", cols(n, xh * 4 + zp, 1), at(z_=zm))

    def cross1(n):
        if CHUNKS[n][2] == "x":
            g1[n]["hp"].wait_recv()
            pass1(n, "fp", cols(n, xh * 4 + z2, 0), at(xh_=ox))
            g1[n]["hm"].wait_recv()
            pass1(n, "fm", cols(n, xh * 4 + z2, 1), at(xh_=ox))
        else:
            g1[n]["qp"].wait_recv()
            pass1(n, "fp", cols(n, ox * 4 + zm, 0), at(z_=zp))
            g1[n]["qm"].wait_recv()
            pass1(n, "fm", cols(n, ox * 4 + zp, 1), at(z_=zm))

    def end1(n):
        for key in ("qp", "qm") if CHUNKS[n][2] == "x" else ("hp", "hm"):
            g1[n][key].wait_recv()
        for key in ("fp", "fm"):
            g1[n][key].wait_recv()
        h, k, _ = CHUNKS[n]
        lanes = pl.ds(h * 384, 384)

        def body(b, carry):
            hi, lo = split(acol[b, :, :, lanes].reshape(BS, 384))
            at_ = pl.ds(pl.multiple_of(b * BS, BS), BS)
            bhi[at_, lanes] = hi
            blo[at_, lanes] = lo
            return carry

        lax.fori_loop(k * 12, k * 12 + 12, body, 0)

    g2 = [{}, {}]

    def rows(n, slot, part=None):
        where = slice(None) if part is None else pl.ds(part * 48, 48)
        return lhs.at[slot, where, pl.ds(n * 1536, 1536)]

    def pass2(n, key, ref, dev):
        g2[n][key] = send(ref, ref, dev)

    def start2(n):
        pass2(n, "yp", rows(n, piece), at(y_=yp))
        pass2(n, "ym", rows(n, piece), at(y_=ym))
        pass2(n, "c", rows(n, piece), at(c_=oc))

    def relay2(n):
        g2[n]["yp"].wait_recv()
        pass2(n, "hp", rows(n, ym * 2 + c, 0), at(y_=yp))
        pass2(n, "cyp", rows(n, ym * 2 + c), at(c_=oc))
        g2[n]["ym"].wait_recv()
        pass2(n, "hm", rows(n, yp * 2 + c, 1), at(y_=ym))
        pass2(n, "cym", rows(n, yp * 2 + c), at(c_=oc))

    def far2(n):
        g2[n]["hp"].wait_recv()
        pass2(n, "chp", rows(n, y2 * 2 + c, 0), at(c_=oc))
        g2[n]["hm"].wait_recv()
        pass2(n, "chm", rows(n, y2 * 2 + c, 1), at(c_=oc))

    def end2(n):
        for key in ("c", "cyp", "cym", "chp", "chm"):
            g2[n][key].wait_recv()

    s1 = []

    def other(there):
        m = pl.ds(there * 192, 192)
        lanes = pl.ds(384, 384)
        for n in range(2):
            k = pl.ds(n * 1536, 1536)
            got = dot3(lhs[pl.ds(there * 2, 2), :, k].reshape(192, 1536), bhi[k, lanes], blo[k, lanes])
            so[m, :] = got if n == 0 else so[m, :] + got
        s1.append(send(so.at[m], rs1.at[m], at(xl_=ol)))

    def own_rows(r, n):
        k = pl.ds(n * 1536, 1536)
        a = lhs[pl.ds(r * PIECES, PIECES), :, k].reshape(ROWS, 1536)
        return dot3(a, bhi[k, pl.ds(0, 384)], blo[k, pl.ds(0, 384)])

    deal1(OTHER)
    deal2()
    arrive1(OTHER)
    start1(0)
    start1(1)
    deal1(OWN)
    relay1(0)
    arrive1(OWN)
    arrive2()
    start2(0)
    start2(1)
    relay1(1)
    start1(2)
    cross1(0)
    relay2(0)
    relay1(2)
    start1(3)
    cross1(1)
    end1(0)
    relay2(1)
    far2(0)
    end1(1)
    cross1(2)
    relay1(3)
    far2(1)
    cross1(3)
    end2(0)
    end2(1)
    other(0)
    other(1)
    other(2)
    other(3)
    end1(2)

    def first_half(i, carry):
        m = pl.ds(pl.multiple_of(i * 192, 64), 192)
        k = pl.ds(0, 1536)
        a = lhs[pl.ds(i * 2, 2), :, k].reshape(192, 1536)
        sw[m, :] = dot3(a, bhi[k, pl.ds(0, 384)], blo[k, pl.ds(0, 384)])
        return carry

    lax.fori_loop(0, 4, first_half, 0)
    end1(3)

    mine = pl.multiple_of(piece * 384, 128)
    block = col * 3
    keep_sq = [[mask_sq[row * 6 + b, block + j].astype(F32) for j in range(3)] for b in range(6)]
    keep_cube = [[mask_cube[row * 6 + b, block + j].astype(F32) for j in range(3)] for b in range(6)]
    diag_sq = [3.0 * mask_sq[row * 6 + b, row * 6 + b].astype(F32) for b in range(6)]
    diag_cube = [2.0 * mask_cube[row * 6 + b, row * 6 + b].astype(F32) for b in range(6)]
    g3 = [{} for _ in range(RC)]
    s2 = [None] * RC

    def pass3(r, key, ref, dev):
        g3[r][key] = send(ref, ref, dev)

    def begin3(r):
        m = pl.ds(r * ROWS, ROWS)
        got = own_rows(r, 1) + sw[m, :]
        if r % (RC // 4) == 0:
            s1[r * 4 // RC].wait_recv()
        got = got + rs1[m, :]
        total = jnp.zeros((8, BS), F32)
        for i in range(PIECES):
            for b in range(6):
                for j in range(3):
                    first, lanes = i * 96 + b * 16, pl.ds(j * BS, BS)
                    s = got[first:first + 16, j * BS:(j + 1) * BS] * keep_sq[b][j]
                    sfull[piece, pl.ds(r * ROWS + first, 16), lanes] = s
                    a = lhs[r * PIECES + i, pl.ds(b * 16, 16), pl.ds(pl.multiple_of(mine + j * BS, BS), BS)]
                    part = a * (a * diag_sq[b] - s * diag_cube[b])
                    total = total + part[0:8] + part[8:16]
        tacc[...] = total if r == 0 else tacc[...] + total
        ref = sfull.at[piece, m]
        pass3(r, "yp", ref, at(y_=yp))
        pass3(r, "ym", ref, at(y_=ym))
        pass3(r, "c", ref, at(c_=oc))

    def square(r, slot, part=None):
        first, count = (r * ROWS, ROWS) if part is None else (r * ROWS + part * (ROWS // 2), ROWS // 2)
        return sfull.at[slot, pl.ds(first, count)]

    def relay3(r):
        g3[r]["yp"].wait_recv()
        pass3(r, "hp", square(r, ym * 2 + c, 0), at(y_=yp))
        g3[r]["ym"].wait_recv()
        pass3(r, "hm", square(r, yp * 2 + c, 1), at(y_=ym))
        pass3(r, "cyp", square(r, ym * 2 + c), at(c_=oc))
        pass3(r, "cym", square(r, yp * 2 + c), at(c_=oc))

    def far3(r):
        g3[r]["hp"].wait_recv()
        g3[r]["hm"].wait_recv()
        pass3(r, "cfar", square(r, y2 * 2 + c), at(c_=oc))

    def cube(r):
        m = pl.ds(r * ROWS, ROWS)
        for key in ("c", "cyp", "cym", "cfar"):
            g3[r][key].wait_recv()

        def body(h, carry):
            lanes = pl.ds(pl.multiple_of(384 - h * 384, 128), 384)
            acc = jnp.zeros((ROWS, 384), F32)
            for s in range(8):
                k = pl.ds(s * 384, 384)
                acc = acc + dot3(sfull[s, m, :], bhi[k, lanes], blo[k, lanes])
            cacc[m, lanes] = acc
            return carry

        lax.fori_loop(0, 2, body, 0)
        s2[r] = send(cacc.at[m, pl.ds(384, 384)], rs2.at[m], at(xl_=ol))

    def finish(r):
        m = pl.ds(r * ROWS, ROWS)
        s2[r].wait_recv()
        got = cacc[m, pl.ds(0, 384)] + rs2[m, :]
        for i in range(PIECES):
            for j in range(3):
                parts = []
                for b in range(6):
                    first = i * 96 + b * 16
                    parts.append(got[first:first + 16, j * BS:(j + 1) * BS] * (2.0 * keep_cube[b][j]))
                s = sfull[piece, pl.ds(r * ROWS + i * 96, 96), pl.ds(j * BS, BS)]
                flat2 = 3.0 * s - jnp.concatenate(parts, axis=0)
                t2recv[pl.ds(j * 768 + r * PIECES + i, 96, stride=8), :] = flat2

    across = [at(xl_=a, y_=b, c_=e) for a, b, e in group1]
    along = [at(xh_=a, z_=b) for a, b in ((xh, zp), (xh, zm), (ox, z), (xh, z2), (ox, zp), (ox, zm), (ox, z2))]
    sums = []

    def trace_first():
        tone[col] = tacc[...]
        sums.append([send(tone.at[col], tone.at[col], dev) for dev in across])

    def trace_second():
        for copy in sums[0]:
            copy.wait_recv()
        ttwo[row] = jnp.sum(tone[...], axis=0)
        sums.append([send(ttwo.at[row], ttwo.at[row], dev) for dev in along])

    def trace_third():
        for copy in sums[1]:
            copy.wait_recv()
        trace[0, 0] = jnp.sum(ttwo[...])

    begin3(0)
    begin3(1)
    for t in range(RC + 3):
        if t < RC:
            relay3(t)
        if t + 2 < RC:
            begin3(t + 2)
        if 0 <= t - 1 < RC:
            far3(t - 1)
        if t == RC - 2:
            trace_first()
        if 0 <= t - 2 < RC:
            cube(t - 2)
        if t == RC + 1:
            trace_second()
        if 0 <= t - 3 < RC:
            finish(t - 3)
    for j in range(3):
        out[:, pl.ds(j * BS, BS)] = t2recv[pl.ds(j * 768, 768), :]
    trace_third()
    assert len(copies) == N_COPIES
    for copy in copies:
        copy.wait_send()


N_COPIES = 45 + 9 * len(CHUNKS) + 2 * 9 + 4 + RC * 9 + 22


def call(den, mask_in, mask_sq, mask_cube):
    vmem = pl.BlockSpec(memory_space=pltpu.VMEM)
    smem = pl.BlockSpec(memory_space=pltpu.SMEM)
    return pl.pallas_call(
        kernel,
        out_shape=(jax.ShapeDtypeStruct((768, 384), F32), jax.ShapeDtypeStruct((1, 1), F32)),
        in_specs=[pl.BlockSpec(memory_space=pl.ANY), smem, smem, smem],
        out_specs=(vmem, smem),
        scratch_shapes=[
            pltpu.VMEM((NB, 6144), F32),
            pltpu.VMEM((2, 16, 24, 384), F32),
            pltpu.VMEM((2304, BS), F32),
            pltpu.VMEM((2304, BS), F32),
            pltpu.VMEM((1152, BS), F32),
            pltpu.VMEM((24, 8, 16, 768), F32),
            pltpu.VMEM((8, 96, HALF), F32),
            pltpu.VMEM((HALF, 768), BF16),
            pltpu.VMEM((HALF, 768), BF16),
            pltpu.VMEM((768, 384), F32),
            pltpu.VMEM((768, 384), F32),
            pltpu.VMEM((768, 384), F32),
            pltpu.VMEM((8, 768, 384), F32),
            pltpu.VMEM((768, 768), F32),
            pltpu.VMEM((768, 384), F32),
            pltpu.VMEM((8, BS), F32),
            pltpu.VMEM((16, 8, BS), F32),
            pltpu.VMEM((8, 8, BS), F32),
            pltpu.SemaphoreType.DMA((N_COPIES,)),
            pltpu.SemaphoreType.DMA((N_COPIES,)),
            pltpu.SemaphoreType.DMA((4,)),
        ],
        compiler_params=pltpu.CompilerParams(
            collective_id=0, has_side_effects=True, vmem_limit_bytes=62 * 2**20
        ),
        cost_estimate=pl.CostEstimate(flops=2 * 768 * 768 * HALF * 6, bytes_accessed=4 * 2**20, transcendentals=0),
    )(den, mask_in, mask_sq, mask_cube)


def shards(density_cyclic, mask_in, mask_sq, mask_cube):
    purified, trace = call(density_cyclic, mask_in, mask_sq, mask_cube)
    return purified, trace[0, 0]


def solution(mesh):
    in_specs = (P(("row", "col"), None), P(), P(), P())
    out_specs = (P("row", "col"), P())
    return jax.shard_map(shards, mesh=mesh, in_specs=in_specs, out_specs=out_specs, check_vma=False)
```

```python
import jax
import jax.numpy as jnp
from jax import lax
from jax.experimental import pallas as pl
from jax.experimental.pallas import tpu as pltpu
from jax.sharding import PartitionSpec as P

F32 = jnp.float32
BF16 = jnp.bfloat16
MESH = pl.DeviceIdType.MESH
BS = 128
NB = 48
HALF = 3072
OWN, OTHER = 0, 1
CHUNKS = ((OTHER, 0, "x"), (OTHER, 1, "x"), (OWN, 0, "z"), (OWN, 1, "z"))
RC = 8
ROWS = 768 // RC
PIECES = 8 // RC


def split(x):
    hi = x.astype(BF16)
    return hi, (x - hi.astype(F32)).astype(BF16)


def dot(a, b):
    return jnp.dot(a, b, preferred_element_type=F32)


def dot3(a, bh, bl):
    ah, al = split(a)
    n = a.shape[0]
    both = dot(jnp.concatenate([ah, al], axis=0), bh)
    return both[:n] + (both[n:] + dot(ah, bl))


def kernel(
    den, mask_in, mask_sq, mask_cube, out, trace,
    local, t1recv, t2src, t2recv, flat, acol, lhs, bhi, blo, so, sw, rs1, sfull, cacc, rs2, tacc, tone, ttwo,
    ss, rs, ls,
):
    row = lax.axis_index("row")
    col = lax.axis_index("col")
    xh, z = row // 4, row % 4
    xl, y, c = col // 8, (col // 2) % 4, col % 2
    piece = col % 8

    def at(xh_=xh, xl_=xl, y_=y, z_=z, c_=c):
        return (xh_ * 4 + z_, (xl_ * 4 + y_) * 2 + c_)

    zp, zm, z2 = (z + 1) % 4, (z + 3) % 4, (z + 2) % 4
    yp, ym, y2 = (y + 1) % 4, (y + 3) % 4, (y + 2) % 4
    ox, ol, oc = 1 - xh, 1 - xl, 1 - c

    group1 = [
        ((xl + a) % 2, (y + b) % 4, (c + e) % 2)
        for b in (2, 1, 3, 0) for a in (1, 0) for e in range(2) if (a, b, e) != (0, 0, 0)
    ]
    group2 = [
        ((xh + a) % 2, (xl + b) % 2, (z + e) % 4)
        for e in (2, 1, 3, 0) for a in (1, 0) for b in (1, 0) if (a, b, e) != (0, 0, 0)
    ]
    partners = [at(xl_=a, y_=b, c_=e) for a, b, e in group1]
    partners += [at(xh_=a, xl_=b, z_=e) for a, b, e in group2[:-1]]

    stage = pltpu.make_async_copy(den, local, ls.at[0])
    stage.start()
    barrier = pltpu.get_barrier_semaphore()
    for dev in partners:
        pl.semaphore_signal(barrier, inc=1, device_id=dev, device_id_type=MESH)
    stage.wait()

    def spread(b, carry):
        for j in range(NB):
            first = (j // 24 * NB + b * 8) * 24 + j % 24
            t2src[pl.ds(first, 8, stride=24), :] = local[pl.ds(pl.multiple_of(b * 8, 8), 8), pl.ds(j * BS, BS)]
        return carry

    lax.fori_loop(0, 6, spread, 0)
    pl.semaphore_wait(barrier, len(partners))

    copies = []

    def send(src, dst, dev):
        i = len(copies)
        copy = pltpu.make_async_remote_copy(
            src_ref=src, dst_ref=dst, send_sem=ss.at[i], recv_sem=rs.at[i], device_id=dev, device_id_type=MESH
        )
        copy.start()
        copies.append(copy)
        return copy

    def part1(h, a, b, e):
        half = a if h == OWN else 1 - a
        first = (half * 4 + b) * 768 + e * 384
        return den.at[pl.ds(pl.multiple_of(a * 24, 8), 24), pl.ds(pl.multiple_of(first, 128), 384)]

    def lines(n):
        return pl.ds(pl.multiple_of(n * 144, 8), 144)

    def part2(a, b, e):
        return t2src.at[lines(b * 8 + a * 4 + e)]

    own1, a1 = [None, None], [None, None]

    def deal1(h):
        own1[h] = pltpu.make_async_copy(part1(h, xl, y, c), t1recv.at[h, col], ls.at[1 + h])
        own1[h].start()
        a1[h] = [send(part1(h, a, b, e), t1recv.at[h, col], at(xl_=a, y_=b, c_=e)) for a, b, e in group1]

    a2, own2 = [], []

    def deal2():
        there = lines(row * 2 + xl)
        own2.append(pltpu.make_async_copy(part2(xh, xl, z), t2recv.at[there], ls.at[3]))
        own2[0].start()
        for a, b, e in group2:
            a2.append(send(part2(a, b, e), t2recv.at[there], at(xh_=a, xl_=b, z_=e)))

    def arrive1(h):
        own1[h].wait()
        for copy in a1[h]:
            copy.wait_recv()
        for j in range(3):
            flat[pl.ds(j * 384, 384), :] = t1recv[h, :, :, pl.ds(j * BS, BS)].reshape(384, BS)
        block = ((xl if h == OWN else ol) * 4 + y) * 6 + c * 3

        def body(b, carry):
            for j in range(3):
                keep = mask_in[xl * 24 + b, block + j].astype(F32)
                for g in range(2):
                    got = flat[pl.ds(j * 384 + g * 192 + b, 8, stride=24), :] * keep
                    acol[b, row, pl.ds(g * 8, 8), pl.ds(h * 384 + j * BS, BS)] = got
            return carry

        lax.fori_loop(0, 24, body, 0)

    def arrive2():
        for copy in own2:
            copy.wait()
        for copy in a2:
            copy.wait_recv()

        def body(b, carry):
            for j in range(24):
                keep = mask_in[row * 6 + b, xl * 24 + j].astype(F32)
                for g in range(2):
                    got = t2recv[pl.ds(g * 8 * 144 + b * 24 + j, 8, stride=144), :] * keep
                    lhs[piece, pl.ds(pl.multiple_of(b * 16 + g * 8, 8), 8), pl.ds(j * BS, BS)] = got
            return carry

        lax.fori_loop(0, 6, body, 0)

    g1 = [{} for _ in CHUNKS]

    def cols(n, slot, part=None):
        h, k, _ = CHUNKS[n]
        first, count = (k * 12, 12) if part is None else (k * 12 + part * 6, 6)
        return acol.at[pl.ds(first, count), slot, :, pl.ds(h * 384, 384)]

    def pass1(n, key, ref, dev):
        g1[n][key] = send(ref, ref, dev)

    def start1(n):
        pass1(n, "x", cols(n, row), at(xh_=ox))
        pass1(n, "zp", cols(n, row), at(z_=zp))
        pass1(n, "zm", cols(n, row), at(z_=zm))

    def relay1(n):
        g1[n]["x"].wait_recv()
        pass1(n, "qp", cols(n, ox * 4 + z), at(z_=zp))
        pass1(n, "qm", cols(n, ox * 4 + z), at(z_=zm))
        g1[n]["zp"].wait_recv()
        pass1(n, "hp", cols(n, xh * 4 + zm, 0), at(z_=zp))
        g1[n]["zm"].wait_recv()
        pass1(n, "hm", cols(n, xh * 4 + zp, 1), at(z_=zm))

    def cross1(n):
        if CHUNKS[n][2] == "x":
            g1[n]["hp"].wait_recv()
            pass1(n, "fp", cols(n, xh * 4 + z2, 0), at(xh_=ox))
            g1[n]["hm"].wait_recv()
            pass1(n, "fm", cols(n, xh * 4 + z2, 1), at(xh_=ox))
        else:
            g1[n]["qp"].wait_recv()
            pass1(n, "fp", cols(n, ox * 4 + zm, 0), at(z_=zp))
            g1[n]["qm"].wait_recv()
            pass1(n, "fm", cols(n, ox * 4 + zp, 1), at(z_=zm))

    def end1(n):
        for key in ("qp", "qm") if CHUNKS[n][2] == "x" else ("hp", "hm"):
            g1[n][key].wait_recv()
        for key in ("fp", "fm"):
            g1[n][key].wait_recv()
        h, k, _ = CHUNKS[n]
        lanes = pl.ds(h * 384, 384)

        def body(b, carry):
            hi, lo = split(acol[b, :, :, lanes].reshape(BS, 384))
            at_ = pl.ds(pl.multiple_of(b * BS, BS), BS)
            bhi[at_, lanes] = hi
            blo[at_, lanes] = lo
            return carry

        lax.fori_loop(k * 12, k * 12 + 12, body, 0)

    g2 = [{}, {}]

    def rows(n, slot, part=None):
        where = slice(None) if part is None else pl.ds(part * 48, 48)
        return lhs.at[slot, where, pl.ds(n * 1536, 1536)]

    def pass2(n, key, ref, dev):
        g2[n][key] = send(ref, ref, dev)

    def start2(n):
        pass2(n, "yp", rows(n, piece), at(y_=yp))
        pass2(n, "ym", rows(n, piece), at(y_=ym))
        pass2(n, "c", rows(n, piece), at(c_=oc))

    def relay2(n):
        g2[n]["yp"].wait_recv()
        pass2(n, "hp", rows(n, ym * 2 + c, 0), at(y_=yp))
        g2[n]["ym"].wait_recv()
        pass2(n, "hm", rows(n, yp * 2 + c, 1), at(y_=ym))
        pass2(n, "cyp", rows(n, ym * 2 + c), at(c_=oc))
        pass2(n, "cym", rows(n, yp * 2 + c), at(c_=oc))

    def far2(n):
        g2[n]["hp"].wait_recv()
        pass2(n, "chp", rows(n, y2 * 2 + c, 0), at(c_=oc))
        g2[n]["hm"].wait_recv()
        pass2(n, "chm", rows(n, y2 * 2 + c, 1), at(c_=oc))

    def end2(n):
        for key in ("c", "cyp", "cym", "chp", "chm"):
            g2[n][key].wait_recv()

    s1 = []

    def other(there):
        m = pl.ds(there * 192, 192)
        lanes = pl.ds(384, 384)
        for n in range(2):
            k = pl.ds(n * 1536, 1536)
            got = dot3(lhs[pl.ds(there * 2, 2), :, k].reshape(192, 1536), bhi[k, lanes], blo[k, lanes])
            so[m, :] = got if n == 0 else so[m, :] + got
        s1.append(send(so.at[m], rs1.at[m], at(xl_=ol)))

    def own_rows(r, n):
        k = pl.ds(n * 1536, 1536)
        a = lhs[pl.ds(r * PIECES, PIECES), :, k].reshape(ROWS, 1536)
        return dot3(a, bhi[k, pl.ds(0, 384)], blo[k, pl.ds(0, 384)])

    deal1(OTHER)
    deal2()
    arrive1(OTHER)
    start1(0)
    start1(1)
    deal1(OWN)
    relay1(0)
    arrive1(OWN)
    arrive2()
    start2(0)
    start2(1)
    relay1(1)
    start1(2)
    cross1(0)
    relay2(0)
    relay1(2)
    start1(3)
    cross1(1)
    end1(0)
    relay2(1)
    far2(0)
    end1(1)
    cross1(2)
    relay1(3)
    far2(1)
    end2(0)
    end2(1)
    other(0)
    cross1(3)
    other(1)
    other(2)
    other(3)
    end1(2)

    def first_half(i, carry):
        m = pl.ds(pl.multiple_of(i * 192, 64), 192)
        k = pl.ds(0, 1536)
        a = lhs[pl.ds(i * 2, 2), :, k].reshape(192, 1536)
        sw[m, :] = dot3(a, bhi[k, pl.ds(0, 384)], blo[k, pl.ds(0, 384)])
        return carry

    lax.fori_loop(0, 4, first_half, 0)
    end1(3)

    mine = pl.multiple_of(piece * 384, 128)
    block = col * 3
    keep_sq = [[mask_sq[row * 6 + b, block + j].astype(F32) for j in range(3)] for b in range(6)]
    keep_cube = [[mask_cube[row * 6 + b, block + j].astype(F32) for j in range(3)] for b in range(6)]
    diag_sq = [3.0 * mask_sq[row * 6 + b, row * 6 + b].astype(F32) for b in range(6)]
    diag_cube = [2.0 * mask_cube[row * 6 + b, row * 6 + b].astype(F32) for b in range(6)]
    g3 = [{} for _ in range(RC)]
    s2 = [None] * RC

    def pass3(r, key, ref, dev):
        g3[r][key] = send(ref, ref, dev)

    def begin3(r):
        m = pl.ds(r * ROWS, ROWS)
        got = own_rows(r, 1) + sw[m, :]
        if r % (RC // 4) == 0:
            s1[r * 4 // RC].wait_recv()
        got = got + rs1[m, :]
        total = jnp.zeros((8, BS), F32)
        for i in range(PIECES):
            for b in range(6):
                for j in range(3):
                    first, lanes = i * 96 + b * 16, pl.ds(j * BS, BS)
                    s = got[first:first + 16, j * BS:(j + 1) * BS] * keep_sq[b][j]
                    sfull[piece, pl.ds(r * ROWS + first, 16), lanes] = s
                    a = lhs[r * PIECES + i, pl.ds(b * 16, 16), pl.ds(pl.multiple_of(mine + j * BS, BS), BS)]
                    part = a * (a * diag_sq[b] - s * diag_cube[b])
                    total = total + part[0:8] + part[8:16]
        tacc[...] = total if r == 0 else tacc[...] + total
        ref = sfull.at[piece, m]
        pass3(r, "yp", ref, at(y_=yp))
        pass3(r, "ym", ref, at(y_=ym))
        pass3(r, "c", ref, at(c_=oc))

    def square(r, slot, part=None):
        first, count = (r * ROWS, ROWS) if part is None else (r * ROWS + part * (ROWS // 2), ROWS // 2)
        return sfull.at[slot, pl.ds(first, count)]

    def relay3(r):
        g3[r]["yp"].wait_recv()
        pass3(r, "hp", square(r, ym * 2 + c, 0), at(y_=yp))
        g3[r]["ym"].wait_recv()
        pass3(r, "hm", square(r, yp * 2 + c, 1), at(y_=ym))
        pass3(r, "cyp", square(r, ym * 2 + c), at(c_=oc))
        pass3(r, "cym", square(r, yp * 2 + c), at(c_=oc))

    def far3(r):
        g3[r]["hp"].wait_recv()
        g3[r]["hm"].wait_recv()
        pass3(r, "cfar", square(r, y2 * 2 + c), at(c_=oc))

    def cube(r):
        m = pl.ds(r * ROWS, ROWS)
        for key in ("c", "cyp", "cym", "cfar"):
            g3[r][key].wait_recv()

        def body(h, carry):
            lanes = pl.ds(pl.multiple_of(384 - h * 384, 128), 384)
            acc = jnp.zeros((ROWS, 384), F32)
            for s in range(8):
                k = pl.ds(s * 384, 384)
                acc = acc + dot3(sfull[s, m, :], bhi[k, lanes], blo[k, lanes])
            cacc[m, lanes] = acc
            return carry

        lax.fori_loop(0, 2, body, 0)
        s2[r] = send(cacc.at[m, pl.ds(384, 384)], rs2.at[m], at(xl_=ol))

    def finish(r):
        m = pl.ds(r * ROWS, ROWS)
        s2[r].wait_recv()
        got = cacc[m, pl.ds(0, 384)] + rs2[m, :]
        for i in range(PIECES):
            for j in range(3):
                parts = []
                for b in range(6):
                    first = i * 96 + b * 16
                    parts.append(got[first:first + 16, j * BS:(j + 1) * BS] * (2.0 * keep_cube[b][j]))
                s = sfull[piece, pl.ds(r * ROWS + i * 96, 96), pl.ds(j * BS, BS)]
                flat2 = 3.0 * s - jnp.concatenate(parts, axis=0)
                t2recv[pl.ds(j * 768 + r * PIECES + i, 96, stride=8), :] = flat2

    across = [at(xl_=a, y_=b, c_=e) for a, b, e in group1]
    along = [at(xh_=a, z_=b) for a, b in ((xh, zp), (xh, zm), (ox, z), (xh, z2), (ox, zp), (ox, zm), (ox, z2))]
    sums = []

    def trace_first():
        tone[col] = tacc[...]
        sums.append([send(tone.at[col], tone.at[col], dev) for dev in across])

    def trace_second():
        for copy in sums[0]:
            copy.wait_recv()
        ttwo[row] = jnp.sum(tone[...], axis=0)
        sums.append([send(ttwo.at[row], ttwo.at[row], dev) for dev in along])

    def trace_third():
        for copy in sums[1]:
            copy.wait_recv()
        trace[0, 0] = jnp.sum(ttwo[...])

    begin3(0)
    begin3(1)
    for t in range(RC + 3):
        if t < RC:
            relay3(t)
        if t + 2 < RC:
            begin3(t + 2)
        if 0 <= t - 1 < RC:
            far3(t - 1)
        if t == RC - 2:
            trace_first()
        if 0 <= t - 2 < RC:
            cube(t - 2)
        if t == RC + 1:
            trace_second()
        if 0 <= t - 3 < RC:
            finish(t - 3)
    for j in range(3):
        out[:, pl.ds(j * BS, BS)] = t2recv[pl.ds(j * 768, 768), :]
    trace_third()
    assert len(copies) == N_COPIES
    for copy in copies:
        copy.wait_send()


N_COPIES = 45 + 9 * len(CHUNKS) + 2 * 9 + 4 + RC * 9 + 22


def call(den, mask_in, mask_sq, mask_cube):
    vmem = pl.BlockSpec(memory_space=pltpu.VMEM)
    smem = pl.BlockSpec(memory_space=pltpu.SMEM)
    return pl.pallas_call(
        kernel,
        out_shape=(jax.ShapeDtypeStruct((768, 384), F32), jax.ShapeDtypeStruct((1, 1), F32)),
        in_specs=[pl.BlockSpec(memory_space=pl.ANY), smem, smem, smem],
        out_specs=(vmem, smem),
        scratch_shapes=[
            pltpu.VMEM((NB, 6144), F32),
            pltpu.VMEM((2, 16, 24, 384), F32),
            pltpu.VMEM((2304, BS), F32),
            pltpu.VMEM((2304, BS), F32),
            pltpu.VMEM((1152, BS), F32),
            pltpu.VMEM((24, 8, 16, 768), F32),
            pltpu.VMEM((8, 96, HALF), F32),
            pltpu.VMEM((HALF, 768), BF16),
            pltpu.VMEM((HALF, 768), BF16),
            pltpu.VMEM((768, 384), F32),
            pltpu.VMEM((768, 384), F32),
            pltpu.VMEM((768, 384), F32),
            pltpu.VMEM((8, 768, 384), F32),
            pltpu.VMEM((768, 768), F32),
            pltpu.VMEM((768, 384), F32),
            pltpu.VMEM((8, BS), F32),
            pltpu.VMEM((16, 8, BS), F32),
            pltpu.VMEM((8, 8, BS), F32),
            pltpu.SemaphoreType.DMA((N_COPIES,)),
            pltpu.SemaphoreType.DMA((N_COPIES,)),
            pltpu.SemaphoreType.DMA((4,)),
        ],
        compiler_params=pltpu.CompilerParams(
            collective_id=0, has_side_effects=True, vmem_limit_bytes=62 * 2**20
        ),
        cost_estimate=pl.CostEstimate(flops=2 * 768 * 768 * HALF * 6, bytes_accessed=4 * 2**20, transcendentals=0),
    )(den, mask_in, mask_sq, mask_cube)


def shards(density_cyclic, mask_in, mask_sq, mask_cube):
    purified, trace = call(density_cyclic, mask_in, mask_sq, mask_cube)
    return purified, trace[0, 0]


def solution(mesh):
    in_specs = (P(("row", "col"), None), P(), P(), P())
    out_specs = (P("row", "col"), P())
    return jax.shard_map(shards, mesh=mesh, in_specs=in_specs, out_specs=out_specs, check_vma=False)
```
